32 devices in a mesh: grp: 8 (over y, x, core), tp: 4 (over z).
Axes of the slice: x: 2, y: 2, z: 4, core: 2. Of those that a mesh axis runs over, the one named last changes fastest.
Arguments:
- queries: bfloat16 [16, 64, 256, 128], P('grp', 'tp'), may hold values from -8 to 8
- new_kv: bfloat16 [16, 8, 256, 256], P('grp', 'tp'), may hold values from -4.5 to 4.5
- kv_pool: bfloat16 [1024, 8, 128, 256], P(('grp', 'tp')), may hold values from -4.5 to 4.5
- cache_lens: int32 [16], replicated, may hold values from 1 to 7936, 63488 in all
- session_seat: int32 [16], replicated, may hold values from 0 to 15, as said below
- old_slots: int32 [16, 64], replicated, may hold values from 0 to 1023, as said below
- new_slots: int32 [16, 64], replicated, may hold values from 0 to 1023, as said below
Outputs:
- attention: bfloat16 [16, 64, 256, 128], P('grp', 'tp')
- new_pool: bfloat16 [1024, 8, 128, 256], P(('grp', 'tp'))
The draws below stay inside these ranges and needn't reach their ends.
Inputs may be any that keep to these rules, and one draw needn't show every extreme that they name: `session_seat`: A permutation of the sessions. `old_slots`: every pool block appears exactly once. Call the group of session s session_seat[s] // 2; every device of grp+tp holds exactly 4 of its 32 blocks for the sessions of each group. `new_slots`: every pool block appears exactly once, and every device holds exactly 4 blocks for the sessions of each group, as for old_slots.
All inputs are finite; a program needn't handle non-finite values.
Results may differ from the reference program's by a relative error of at most 0.005.
Values may be sent and summed in bfloat16 or wider, within the bound.
A program may use at most 128 MiB of HBM per device.

```python
import math
import jax
import jax.numpy as jnp
import numpy as np
from jax import lax

QH = 64
KVH = 8
HD = 128
BLK = 128
MAXBLK = 64
TURN = 256
SPG = 2
SESS = 16
MAXLEN = 7936
SLOTS = 1024
POOL_DEV = 32


def seat_order(key):
    return jax.random.permutation(jax.random.fold_in(key, 101), SESS).astype(jnp.int32)


def slot_table(key, seat_of_session):
    owners = SESS * MAXBLK // POOL_DEV
    groups = SESS // SPG
    group_share = POOL_DEV // groups
    local_key, group_key = jax.random.split(key)
    local_codes = jax.vmap(lambda subkey: jax.random.permutation(subkey, POOL_DEV))(jax.random.split(local_key, owners))
    local_slot = jnp.argsort(local_codes, axis=1, stable=True).astype(jnp.int32)
    group_codes = jax.vmap(lambda subkey: jax.random.permutation(subkey, SPG * MAXBLK))(jax.random.split(group_key, groups))
    item_of = jnp.argsort(group_codes, axis=1, stable=True).astype(jnp.int32)
    seat_ids = jnp.arange(SESS, dtype=jnp.int32)[:, None]
    block_ids = jnp.arange(MAXBLK, dtype=jnp.int32)[None, :]
    group_of = seat_ids // SPG + 0 * block_ids
    position = seat_ids % SPG * MAXBLK + block_ids
    item = item_of[group_of, position]
    owner = item // group_share
    rank_in = item % group_share
    local = local_slot[owner, group_of * group_share + rank_in]
    by_seat = owner * POOL_DEV + local
    return by_seat[seat_of_session].astype(jnp.int32)


def draw_session_seat(key, part):
    return seat_order(key)


def draw_old_slots(key, part):
    seats = seat_order(key)
    key = jax.random.fold_in(key, 3)
    return slot_table(key, seats)


def draw_new_slots(key, part):
    seats = seat_order(key)
    key = jax.random.fold_in(key, 4)
    return slot_table(key, seats)


def draw_queries(key, part):
    key = jax.random.fold_in(key, 5)
    values = jnp.clip(2.0 * jax.random.normal(key, (SESS, QH, TURN, HD), jnp.float32), -8.0, 8.0)
    return values.astype(jnp.bfloat16)


def draw_new_kv(key, part):
    key = jax.random.fold_in(key, 6)
    values = jnp.clip(jax.random.normal(key, (SESS, KVH, TURN, 2 * HD), jnp.float32), -4.5, 4.5)
    return values.astype(jnp.bfloat16)


def level_of(own_key, shape, pieces, low, high):
    def one(axis_at, parts):
        steps = jax.random.uniform(jax.random.fold_in(jax.random.fold_in(own_key, 6), axis_at), (parts,), jnp.float32, low / len(pieces), high / len(pieces))
        return jnp.repeat(jnp.exp(steps), shape[axis_at] // parts).reshape((-1,) + (1,) * (len(shape) - axis_at - 1))

    level = one(*pieces[0])
    for cut in pieces[1:]:
        level = level * one(*cut)
    return level


def length_profile(number_of, total, limit, lean):
    loads = [(1 << 20) // math.isqrt(grade ** lean) + 1 for grade in range(2, number_of + 1)]
    spare, given = total - limit - (number_of - 1), [1] * (number_of - 1)
    while spare > 0:
        candidates = [i for i in range(number_of - 1) if given[i] < limit]
        whole, left = sum([loads[i] for i in candidates]), spare
        for i in candidates:
            more = min(limit - given[i], max(1, left * loads[i] // whole), spare)
            given[i] = given[i] + more
            spare = spare - more
    return np.array([limit] + given)


def ragged(own_key, count, total, most, slope):
    if count == 2:
        one = jax.random.randint(own_key, (), max(1, total - most), min(most, total - 1) + 1)
        return jnp.stack([one, total - one])
    lengths = jnp.asarray(length_profile(count, total, most, slope), jnp.int32)
    pairs = (count - 1) // 2
    source_of, sink = lengths[1:1 + 2 * pairs:2], lengths[2:2 + 2 * pairs:2]
    margin = jnp.minimum(source_of - 1, most - sink)
    moved = jax.random.randint(jax.random.fold_in(own_key, 1), (pairs,), 0, 1 << 20) % (margin + 1)
    lengths = lengths.at[1:1 + 2 * pairs:2].set(source_of - moved).at[2:2 + 2 * pairs:2].set(sink + moved)
    return lengths[jax.random.permutation(jax.random.fold_in(own_key, 2), count)]


def normal_values(own_key, extent, scale, bound, pieces=(), kind=jnp.bfloat16):
    entries = scale * jax.random.normal(own_key, extent, jnp.float32)
    if pieces:
        entries = entries * level_of(own_key, extent, pieces, -0.22, 0.18)
    return jnp.clip(entries, -bound, bound).astype(kind)


def setup_inputs(seed: int = 0) -> dict:
    keys = jax.random.split(jax.random.key(seed), 8)
    return {
        "queries": draw_queries(jax.random.fold_in(keys[7], 71), 0),
        "new_kv": draw_new_kv(jax.random.fold_in(keys[7], 71), 0),
        "kv_pool": normal_values(keys[2], (SLOTS, KVH, BLK, 2 * HD), 1.0, 4.5, ((0, 32),)),
        "cache_lens": ragged(keys[3], SESS, SESS * MAXLEN // 2, MAXLEN, 2).astype(jnp.int32),
        "session_seat": draw_session_seat(jax.random.fold_in(keys[7], 71), 0),
        "old_slots": draw_old_slots(jax.random.fold_in(keys[7], 71), 0),
        "new_slots": draw_new_slots(jax.random.fold_in(keys[7], 71), 0),
    }


def reference(queries, new_kv, kv_pool, cache_lens, session_seat, old_slots, new_slots):
    seat_session = jnp.zeros((SESS,), jnp.int32).at[session_seat].set(jnp.arange(SESS, dtype=jnp.int32))
    seat_lens = cache_lens[seat_session].astype(jnp.int32)
    old_table = old_slots[seat_session]
    new_table = new_slots[seat_session]
    key_span = MAXBLK * BLK
    group_size = QH // KVH

    def restore(inputs):
        table_row, length, fresh_kv = inputs
        blocks = kv_pool[table_row]
        cached = jnp.transpose(blocks, (1, 0, 2, 3)).reshape(KVH, key_span, 2 * HD)
        position = jnp.arange(key_span, dtype=jnp.int32)
        cached = jnp.where(position[None, :, None] < length, cached, jnp.zeros((), cached.dtype))
        zero_index = jnp.zeros((), jnp.int32)
        return lax.dynamic_update_slice(cached, fresh_kv, (zero_index, length.astype(jnp.int32), zero_index))

    grown_cache = lax.map(restore, (old_table, seat_lens, new_kv))

    def attend_seat(inputs):
        seat_queries, seat_grown, length = inputs
        turn_index = jnp.arange(group_size * TURN, dtype=jnp.int32) % TURN
        limits = length + turn_index
        column = jnp.arange(key_span, dtype=jnp.int32)

        def attend_head(head_inputs):
            head_queries, head_grown = head_inputs
            query_rows = head_queries.reshape(group_size * TURN, HD)
            scores = jnp.dot(query_rows, head_grown[:, :HD].T, preferred_element_type=jnp.float32) * (HD ** -0.5)
            scores = jnp.where(column[None, :] <= limits[:, None], scores, -1e30)
            highest = jnp.max(scores, axis=1, keepdims=True)
            weights = jnp.exp(scores - highest)
            weights = (weights / jnp.sum(weights, axis=1, keepdims=True)).astype(jnp.bfloat16)
            summed = jnp.dot(weights, head_grown[:, HD:], preferred_element_type=jnp.float32)
            return summed.astype(jnp.bfloat16).reshape(group_size, TURN, HD)

        return lax.map(attend_head, (seat_queries.reshape(KVH, group_size, TURN, HD), seat_grown))

    attention = lax.map(attend_seat, (queries, grown_cache, seat_lens)).reshape(SESS, QH, TURN, HD)
    grown_blocks = grown_cache.reshape(SESS, KVH, MAXBLK, BLK, 2 * HD)
    grown_blocks = jnp.transpose(grown_blocks, (0, 2, 1, 3, 4)).reshape(SESS * MAXBLK, KVH, BLK, 2 * HD)
    new_pool = jnp.zeros((SLOTS, KVH, BLK, 2 * HD), jnp.bfloat16).at[new_table.reshape(-1)].set(grown_blocks)
    return attention, new_pool
```

```python
import functools

import jax
import jax.numpy as jnp
from jax import lax
from jax.experimental import pallas as pl
from jax.experimental.pallas import tpu as pltpu
from jax.sharding import PartitionSpec as P

VMEM_LIMIT = 50 * 1024 * 1024


def merge_kernel(lanes, block_len, rows_ref, cut_ref, fresh_ref, *refs):
    cached_refs, fresh, out = refs[:lanes], refs[lanes], refs[lanes + 1]
    step = pl.program_id(0)
    for lane in range(lanes):
        cached = cached_refs[lane]
        cut = cut_ref[step * lanes + lane]
        fill = fresh_ref[step * lanes + lane]

        @pl.when(cut == block_len)
        def _():
            out[lane] = cached[0]

        @pl.when(cut == 0)
        def _():
            out[lane] = fresh[fill]

        @pl.when(jnp.logical_and(cut > 0, cut < block_len))
        def _():
            row = lax.broadcasted_iota(jnp.int32, cached.shape[1:], 0)
            out[lane] = jnp.where(
                row < cut, cached[0].astype(jnp.float32), fresh[fill].astype(jnp.float32)
            ).astype(out.dtype)


def merge(received, fresh, rows, cut, fill):
    total, block_len, width = received.shape
    lanes = 8
    spec = lambda lane: pl.BlockSpec(
        (1, block_len, width), lambda s, rows, cut, fill: (rows[s * lanes + lane], 0, 0)
    )
    return pl.pallas_call(
        functools.partial(merge_kernel, lanes, block_len),
        grid_spec=pltpu.PrefetchScalarGridSpec(
            num_scalar_prefetch=3,
            grid=(total // lanes,),
            in_specs=[spec(lane) for lane in range(lanes)]
            + [pl.BlockSpec(fresh.shape, lambda s, *_: (0, 0, 0))],
            out_specs=pl.BlockSpec((lanes, block_len, width), lambda s, *_: (s, 0, 0)),
        ),
        out_shape=jax.ShapeDtypeStruct(received.shape, received.dtype),
        compiler_params=pltpu.CompilerParams(vmem_limit_bytes=VMEM_LIMIT),
        cost_estimate=pl.CostEstimate(
            flops=0, bytes_accessed=4 * total * block_len * width, transcendentals=0
        ),
        name="merge_blocks",
    )(rows, cut, fill, *([received] * lanes), fresh)


def store_kernel(lanes, heads, rows_ref, *refs):
    ins, out = refs[: lanes * heads], refs[-1]
    for lane in range(lanes):
        for head in range(heads):
            out[lane, head, 0] = ins[lane * heads + head][0]


def store(arrived, rows, pool, pool_shape, head_slot):
    unused_total, block_len, width = arrived.shape
    pool_dev, heads = pool_shape[:2]
    lanes = 2
    spec = lambda lane, head: pl.BlockSpec(
        (1, block_len, width),
        lambda s, rows: (rows[(s * lanes + lane) * heads + head], 0, 0),
    )
    in_specs = [spec(lane, head) for lane in range(lanes) for head in range(heads)]
    operands = [arrived] * (lanes * heads)
    aliases = {}
    if pool is not None:
        in_specs.append(pl.BlockSpec(memory_space=pl.ANY))
        operands.append(pool)
        aliases = {len(operands): 0}
    return pl.pallas_call(
        functools.partial(store_kernel, lanes, heads),
        grid_spec=pltpu.PrefetchScalarGridSpec(
            num_scalar_prefetch=1,
            grid=(pool_dev // lanes,),
            in_specs=in_specs,
            out_specs=pl.BlockSpec(
                (lanes, heads, 1, block_len, width), lambda s, rows: (s, 0, head_slot, 0, 0)
            ),
        ),
        out_shape=jax.ShapeDtypeStruct(pool_shape, arrived.dtype),
        input_output_aliases=aliases,
        compiler_params=pltpu.CompilerParams(vmem_limit_bytes=VMEM_LIMIT),
        cost_estimate=pl.CostEstimate(
            flops=0, bytes_accessed=4 * arrived.size, transcendentals=0
        ),
        name="store_blocks",
    )(rows, *operands)


def attend_kernel(pages, block_len, turn, tile, scale, places_ref, lens_ref, *refs):
    page_refs = refs[:pages]
    query, out, total, high, norm = refs[pages:]
    seat, step = pl.program_id(0), pl.program_id(1)
    head_dim, rows = query.shape[1:]
    span = pages * block_len
    length = lens_ref[seat]
    base = step * span
    factor = scale * 1.4426950408889634

    @pl.when(step == 0)
    def _():
        total[...] = jnp.zeros_like(total)
        norm[...] = jnp.zeros_like(norm)
        high[...] = jnp.full_like(high, -1e30)

    def update(masked):
        keys = jnp.concatenate([page[0, :, :head_dim] for page in page_refs], axis=0)
        values = jnp.concatenate([page[0, :, head_dim:] for page in page_refs], axis=0)
        values_t = values.T
        for at in range(0, rows, tile):
            part = pl.ds(at, tile)
            scores = jnp.dot(keys, query[0, :, part], preferred_element_type=jnp.float32)
            if masked:
                column = lax.broadcasted_iota(jnp.int32, scores.shape, 0) + base
                limit = (lax.broadcasted_iota(jnp.int32, scores.shape, 1) + at) % turn + length
                scores = jnp.where(column <= limit, scores, -1e30)
            before = high[:, part]
            now = jnp.maximum(before, jnp.max(scores, axis=0, keepdims=True))
            weights = jnp.exp2((scores - now) * factor)
            fade = jnp.exp2((before - now) * factor)
            high[:, part] = now
            norm[:, part] = norm[:, part] * fade + jnp.sum(weights, axis=0, keepdims=True)
            total[:, part] = total[:, part] * fade + jnp.dot(
                values_t, weights.astype(jnp.bfloat16), preferred_element_type=jnp.float32
            )

    @pl.when(base + span - 1 <= length)
    def _():
        update(False)

    @pl.when(jnp.logical_and(base + span - 1 > length, base < length + turn))
    def _():
        update(True)

    @pl.when(step == pl.num_programs(1) - 1)
    def _():
        out[0] = (total[...] / norm[...]).astype(out.dtype)


def attend(grown, query_t, places, lens, turn, max_blocks):
    seats, head_dim, rows = query_t.shape
    unused_total, block_len, width = grown.shape
    pages = 4
    span = pages * block_len
    steps = max_blocks // pages

    def spec(page):
        def index(seat, step, places, lens):
            last = (lens[seat] + turn - 1) // span
            return (places[seat * max_blocks + jnp.minimum(step, last) * pages + page], 0, 0)

        return pl.BlockSpec((1, block_len, width), index)

    by_seat = pl.BlockSpec((1, head_dim, rows), lambda seat, step, *_: (seat, 0, 0))
    work = seats * rows * max_blocks * block_len
    return pl.pallas_call(
        functools.partial(
            attend_kernel, pages, block_len, turn, min(512, rows), head_dim ** (-0.5)
        ),
        grid_spec=pltpu.PrefetchScalarGridSpec(
            num_scalar_prefetch=2,
            grid=(seats, steps),
            in_specs=[spec(page) for page in range(pages)] + [by_seat],
            out_specs=by_seat,
            scratch_shapes=[
                pltpu.VMEM((head_dim, rows), jnp.float32),
                pltpu.VMEM((1, rows), jnp.float32),
                pltpu.VMEM((1, rows), jnp.float32),
            ],
        ),
        out_shape=jax.ShapeDtypeStruct(query_t.shape, query_t.dtype),
        compiler_params=pltpu.CompilerParams(vmem_limit_bytes=VMEM_LIMIT),
        cost_estimate=pl.CostEstimate(
            flops=4 * work * head_dim, bytes_accessed=2 * grown.size, transcendentals=work
        ),
        name="attend_head",
    )(places, lens, *([grown] * pages), query_t)


def pool_places(slots, session_group, my_index, pool_dev, share):
    mine = my_index * pool_dev + jnp.arange(pool_dev, dtype=jnp.int32)
    match = slots[None] == mine[:, None, None]
    group = jnp.sum(jnp.where(match, session_group[None, :, None], 0), axis=(1, 2))
    local = jnp.arange(pool_dev, dtype=jnp.int32)
    earlier = jnp.logical_and(group[None, :] == group[:, None], local[None, :] < local[:, None])
    return group, jnp.sum(earlier.astype(jnp.int32), axis=1)


def group_places(table, pool_dev, share):
    slots = table.reshape(-1)
    owner = slots // pool_dev
    earlier = jnp.logical_and(owner[None, :] == owner[:, None], slots[None, :] < slots[:, None])
    return owner * share + jnp.sum(earlier.astype(jnp.int32), axis=1)


def local(queries, new_kv, kv_pool, cache_lens, session_seat, old_slots, new_slots):
    group_count = lax.axis_size("grp")
    tp_count = lax.axis_size("tp")
    owners = group_count * tp_count
    pool_dev, kv_heads, block_len, width = kv_pool.shape
    head_dim = width // 2
    seats, qh_dev, turn, unused_dim = queries.shape
    kvh_dev = new_kv.shape[1]
    group_size = qh_dev // kvh_dev
    max_blocks = old_slots.shape[1]
    share = pool_dev // group_count
    group_index = lax.axis_index("grp")
    my_index = group_index * tp_count + lax.axis_index("tp")
    session_group = session_seat // seats

    group, rank = pool_places(old_slots, session_group, my_index, pool_dev, share)
    locals_ = jnp.arange(pool_dev, dtype=jnp.int32)
    order = jnp.sum(
        jnp.where((group * share + rank)[None, :] == locals_[:, None], locals_[None, :], 0), axis=1
    )
    pick = jnp.repeat(order.reshape(group_count, 1, share), tp_count, axis=1)
    head = jnp.arange(tp_count, dtype=jnp.int32)[None, :, None] * kvh_dev
    first_row = (pick * kv_heads + head).reshape(owners, share)
    pool_rows = kv_pool.reshape(pool_dev * kv_heads, block_len, width)

    seat_ids = group_index * seats + jnp.arange(seats, dtype=jnp.int32)
    here = session_seat[None, :] == seat_ids[:, None]
    lens = jnp.sum(jnp.where(here, cache_lens[None, :], 0), axis=1)
    old_table = jnp.sum(jnp.where(here[:, :, None], old_slots[None], 0), axis=1)
    new_table = jnp.sum(jnp.where(here[:, :, None], new_slots[None], 0), axis=1)
    arrival = group_places(old_table, pool_dev, share)
    leave = group_places(new_table, pool_dev, share)
    block = jnp.arange(max_blocks, dtype=jnp.int32)[None, :]
    fresh_blocks = turn // block_len + 2
    cut = jnp.clip(lens[:, None] - block * block_len, 0, block_len)
    beyond = block - lens[:, None] // block_len
    beyond = jnp.where(
        jnp.logical_and(beyond >= 0, beyond < fresh_blocks - 1), beyond, fresh_blocks - 1
    )
    fill = beyond + fresh_blocks * jnp.arange(seats, dtype=jnp.int32)[:, None]
    at = leave[None, :] == jnp.arange(seats * max_blocks, dtype=jnp.int32)[:, None]
    by_leave = lambda per_block: jnp.sum(jnp.where(at, per_block.reshape(1, -1), 0), axis=1)
    merge_rows, merge_cut, merge_fill = by_leave(arrival), by_leave(cut), by_leave(fill)

    blank = jnp.zeros((kvh_dev, fresh_blocks * block_len, width), new_kv.dtype)
    fresh = jnp.stack(
        [
            lax.dynamic_update_slice(blank, new_kv[seat], (0, lens[seat] % block_len, 0))
            for seat in range(seats)
        ]
    ).reshape(seats, kvh_dev, fresh_blocks, block_len, width)

    new_group, new_rank = pool_places(new_slots, session_group, my_index, pool_dev, share)
    sender = new_group[:, None] * tp_count + jnp.arange(tp_count, dtype=jnp.int32)[None, :]
    store_rows = (sender * share + new_rank[:, None]).reshape(-1)

    query_t = jnp.swapaxes(
        queries.reshape(seats, kvh_dev, group_size * turn, head_dim), 2, 3
    )
    received = [
        lax.all_to_all(
            pool_rows[first_row + slot], ("grp", "tp"), split_axis=0, concat_axis=0, tiled=True
        )
        for slot in range(kvh_dev)
    ]
    grown, arrived, outputs = [], [], []
    for slot in range(kvh_dev):
        grown.append(
            merge(
                received[slot].reshape(owners * share, block_len, width),
                fresh[:, slot].reshape(seats * fresh_blocks, block_len, width),
                merge_rows,
                merge_cut,
                merge_fill,
            )
        )
        arrived.append(
            lax.all_to_all(
                grown[slot].reshape(owners, share, block_len, width),
                ("grp", "tp"),
                split_axis=0,
                concat_axis=0,
                tiled=True,
            )
        )
    for slot in range(kvh_dev):
        result = attend(grown[slot], query_t[:, slot], leave, lens, turn, max_blocks)
        outputs.append(jnp.swapaxes(result, 1, 2).reshape(seats, group_size, turn, head_dim))
    attention = jnp.concatenate(outputs, axis=1)
    pool = None
    pool_shape = (pool_dev, tp_count, kvh_dev, block_len, width)
    for slot in range(kvh_dev):
        blocks = arrived[slot].reshape(owners * share, block_len, width)
        pool = store(blocks, store_rows, pool, pool_shape, slot)
    return (attention, pool.reshape(kv_pool.shape))


def solution(mesh):
    in_specs = (
        P("grp", "tp", None, None),
        P("grp", "tp", None, None),
        P(("grp", "tp"), None, None, None),
        P(),
        P(),
        P(),
        P(),
    )
    out_specs = (P("grp", "tp", None, None), P(("grp", "tp"), None, None, None))
    return jax.shard_map(local, mesh=mesh, in_specs=in_specs, out_specs=out_specs, check_vma=False)
```

```python
import functools

import jax
import jax.numpy as jnp
from jax import lax
from jax.experimental import pallas as pl
from jax.experimental.pallas import tpu as pltpu
from jax.sharding import PartitionSpec as P

VMEM_LIMIT = 50 * 1024 * 1024


def merge_kernel(lanes, block_len, rows_ref, cut_ref, fresh_ref, *refs):
    cached_refs, fresh, out = refs[:lanes], refs[lanes], refs[lanes + 1]
    step = pl.program_id(0)
    for lane in range(lanes):
        cached = cached_refs[lane]
        cut = cut_ref[step * lanes + lane]
        fill = fresh_ref[step * lanes + lane]

        @pl.when(cut == block_len)
        def _():
            out[lane] = cached[0]

        @pl.when(cut == 0)
        def _():
            out[lane] = fresh[fill]

        @pl.when(jnp.logical_and(cut > 0, cut < block_len))
        def _():
            row = lax.broadcasted_iota(jnp.int32, cached.shape[1:], 0)
            out[lane] = jnp.where(
                row < cut, cached[0].astype(jnp.float32), fresh[fill].astype(jnp.float32)
            ).astype(out.dtype)


def merge(received, fresh, rows, cut, fill):
    total, block_len, width = received.shape
    lanes = 8
    spec = lambda lane: pl.BlockSpec(
        (1, block_len, width), lambda s, rows, cut, fill: (rows[s * lanes + lane], 0, 0)
    )
    return pl.pallas_call(
        functools.partial(merge_kernel, lanes, block_len),
        grid_spec=pltpu.PrefetchScalarGridSpec(
            num_scalar_prefetch=3,
            grid=(total // lanes,),
            in_specs=[spec(lane) for lane in range(lanes)]
            + [pl.BlockSpec(fresh.shape, lambda s, *_: (0, 0, 0))],
            out_specs=pl.BlockSpec((lanes, block_len, width), lambda s, *_: (s, 0, 0)),
        ),
        out_shape=jax.ShapeDtypeStruct(received.shape, received.dtype),
        compiler_params=pltpu.CompilerParams(vmem_limit_bytes=VMEM_LIMIT),
        cost_estimate=pl.CostEstimate(
            flops=0, bytes_accessed=4 * total * block_len * width, transcendentals=0
        ),
        name="merge_blocks",
    )(rows, cut, fill, *([received] * lanes), fresh)


def take_kernel(count, rows_ref, source, out, done):
    copies = [
        pltpu.make_async_copy(source.at[rows_ref[at]], out.at[at], done.at[at])
        for at in range(count)
    ]
    for copy in copies:
        copy.start()
    for copy in copies:
        copy.wait()


def take(source, rows):
    count = rows.shape[0]
    shape = (count,) + source.shape[1:]
    return pl.pallas_call(
        functools.partial(take_kernel, count),
        grid_spec=pltpu.PrefetchScalarGridSpec(
            num_scalar_prefetch=1,
            grid=(1,),
            in_specs=[pl.BlockSpec(memory_space=pl.ANY)],
            out_specs=pl.BlockSpec(memory_space=pl.ANY),
            scratch_shapes=[pltpu.SemaphoreType.DMA((count,))],
        ),
        out_shape=jax.ShapeDtypeStruct(shape, source.dtype),
        compiler_params=pltpu.CompilerParams(vmem_limit_bytes=VMEM_LIMIT),
        cost_estimate=pl.CostEstimate(
            flops=0, bytes_accessed=4 * count * source.shape[1] * source.shape[2], transcendentals=0
        ),
        name="take_blocks",
    )(rows, source)


def store_kernel(pool_dev, heads, head_slot, rows_ref, arrived, *refs):
    out, done = refs[-2:]
    copies = [
        pltpu.make_async_copy(
            arrived.at[rows_ref[slot * heads + head]],
            out.at[slot, head, head_slot],
            done.at[slot * heads + head],
        )
        for slot in range(pool_dev)
        for head in range(heads)
    ]
    for copy in copies:
        copy.start()
    for copy in copies:
        copy.wait()


def store(arrived, rows, pool, pool_shape, head_slot):
    pool_dev, heads = pool_shape[:2]
    operands = [arrived]
    aliases = {}
    if pool is not None:
        operands.append(pool)
        aliases = {2: 0}
    return pl.pallas_call(
        functools.partial(store_kernel, pool_dev, heads, head_slot),
        grid_spec=pltpu.PrefetchScalarGridSpec(
            num_scalar_prefetch=1,
            grid=(1,),
            in_specs=[pl.BlockSpec(memory_space=pl.ANY)] * len(operands),
            out_specs=pl.BlockSpec(memory_space=pl.ANY),
            scratch_shapes=[pltpu.SemaphoreType.DMA((pool_dev * heads,))],
        ),
        out_shape=jax.ShapeDtypeStruct(pool_shape, arrived.dtype),
        input_output_aliases=aliases,
        compiler_params=pltpu.CompilerParams(vmem_limit_bytes=VMEM_LIMIT),
        cost_estimate=pl.CostEstimate(
            flops=0, bytes_accessed=4 * arrived.size, transcendentals=0
        ),
        name="store_blocks",
    )(rows, *operands)


def attend_kernel(pages, block_len, turn, tile, scale, places_ref, lens_ref, *refs):
    page_refs = refs[:pages]
    query, out, total, high, norm = refs[pages:]
    seat, step = pl.program_id(0), pl.program_id(1)
    head_dim, rows = query.shape[1:]
    span = pages * block_len
    length = lens_ref[seat]
    base = step * span
    factor = scale * 1.4426950408889634

    @pl.when(step == 0)
    def _():
        total[...] = jnp.zeros_like(total)
        norm[...] = jnp.zeros_like(norm)
        high[...] = jnp.full_like(high, -1e30)

    def update(masked):
        keys = jnp.concatenate([page[0, :, :head_dim] for page in page_refs], axis=0)
        values = jnp.concatenate([page[0, :, head_dim:] for page in page_refs], axis=0)
        values_t = values.T
        for at in range(0, rows, tile):
            part = pl.ds(at, tile)
            scores = jnp.dot(keys, query[0, :, part], preferred_element_type=jnp.float32)
            if masked:
                column = lax.broadcasted_iota(jnp.int32, scores.shape, 0) + base
                limit = (lax.broadcasted_iota(jnp.int32, scores.shape, 1) + at) % turn + length
                scores = jnp.where(column <= limit, scores, -1e30)
            before = high[:, part]
            now = jnp.maximum(before, jnp.max(scores, axis=0, keepdims=True))
            weights = jnp.exp2((scores - now) * factor)
            fade = jnp.exp2((before - now) * factor)
            high[:, part] = now
            norm[:, part] = norm[:, part] * fade + jnp.sum(weights, axis=0, keepdims=True)
            total[:, part] = total[:, part] * fade + jnp.dot(
                values_t, weights.astype(jnp.bfloat16), preferred_element_type=jnp.float32
            )

    @pl.when(base + span - 1 <= length)
    def _():
        update(False)

    @pl.when(jnp.logical_and(base + span - 1 > length, base < length + turn))
    def _():
        update(True)

    @pl.when(step == pl.num_programs(1) - 1)
    def _():
        out[0] = (total[...] / norm[...]).astype(out.dtype)


def attend(grown, query_t, places, lens, turn, max_blocks):
    seats, head_dim, rows = query_t.shape
    unused_total, block_len, width = grown.shape
    pages = 4
    span = pages * block_len
    steps = max_blocks // pages

    def spec(page):
        def index(seat, step, places, lens):
            last = (lens[seat] + turn - 1) // span
            return (places[seat * max_blocks + jnp.minimum(step, last) * pages + page], 0, 0)

        return pl.BlockSpec((1, block_len, width), index)

    by_seat = pl.BlockSpec((1, head_dim, rows), lambda seat, step, *_: (seat, 0, 0))
    work = seats * rows * max_blocks * block_len
    return pl.pallas_call(
        functools.partial(
            attend_kernel, pages, block_len, turn, min(512, rows), head_dim ** (-0.5)
        ),
        grid_spec=pltpu.PrefetchScalarGridSpec(
            num_scalar_prefetch=2,
            grid=(seats, steps),
            in_specs=[spec(page) for page in range(pages)] + [by_seat],
            out_specs=by_seat,
            scratch_shapes=[
                pltpu.VMEM((head_dim, rows), jnp.float32),
                pltpu.VMEM((1, rows), jnp.float32),
                pltpu.VMEM((1, rows), jnp.float32),
            ],
        ),
        out_shape=jax.ShapeDtypeStruct(query_t.shape, query_t.dtype),
        compiler_params=pltpu.CompilerParams(vmem_limit_bytes=VMEM_LIMIT),
        cost_estimate=pl.CostEstimate(
            flops=4 * work * head_dim, bytes_accessed=2 * grown.size, transcendentals=work
        ),
        name="attend_head",
    )(places, lens, *([grown] * pages), query_t)


def pool_places(slots, session_group, my_index, pool_dev, share):
    mine = my_index * pool_dev + jnp.arange(pool_dev, dtype=jnp.int32)
    match = slots[None] == mine[:, None, None]
    group = jnp.sum(jnp.where(match, session_group[None, :, None], 0), axis=(1, 2))
    local = jnp.arange(pool_dev, dtype=jnp.int32)
    earlier = jnp.logical_and(group[None, :] == group[:, None], local[None, :] < local[:, None])
    return group, jnp.sum(earlier.astype(jnp.int32), axis=1)


def group_places(table, pool_dev, share):
    slots = table.reshape(-1)
    owner = slots // pool_dev
    earlier = jnp.logical_and(owner[None, :] == owner[:, None], slots[None, :] < slots[:, None])
    return owner * share + jnp.sum(earlier.astype(jnp.int32), axis=1)


def local(queries, new_kv, kv_pool, cache_lens, session_seat, old_slots, new_slots):
    group_count = lax.axis_size("grp")
    tp_count = lax.axis_size("tp")
    owners = group_count * tp_count
    pool_dev, kv_heads, block_len, width = kv_pool.shape
    head_dim = width // 2
    seats, qh_dev, turn, unused_dim = queries.shape
    kvh_dev = new_kv.shape[1]
    group_size = qh_dev // kvh_dev
    max_blocks = old_slots.shape[1]
    share = pool_dev // group_count
    group_index = lax.axis_index("grp")
    my_index = group_index * tp_count + lax.axis_index("tp")
    session_group = session_seat // seats

    group, rank = pool_places(old_slots, session_group, my_index, pool_dev, share)
    locals_ = jnp.arange(pool_dev, dtype=jnp.int32)
    order = jnp.sum(
        jnp.where((group * share + rank)[None, :] == locals_[:, None], locals_[None, :], 0), axis=1
    )
    pick = jnp.repeat(order.reshape(group_count, 1, share), tp_count, axis=1)
    head = jnp.arange(tp_count, dtype=jnp.int32)[None, :, None] * kvh_dev
    first_row = (pick * kv_heads + head).reshape(owners, share)
    pool_rows = kv_pool.reshape(pool_dev * kv_heads, block_len, width)

    seat_ids = group_index * seats + jnp.arange(seats, dtype=jnp.int32)
    here = session_seat[None, :] == seat_ids[:, None]
    lens = jnp.sum(jnp.where(here, cache_lens[None, :], 0), axis=1)
    old_table = jnp.sum(jnp.where(here[:, :, None], old_slots[None], 0), axis=1)
    new_table = jnp.sum(jnp.where(here[:, :, None], new_slots[None], 0), axis=1)
    arrival = group_places(old_table, pool_dev, share)
    leave = group_places(new_table, pool_dev, share)
    block = jnp.arange(max_blocks, dtype=jnp.int32)[None, :]
    fresh_blocks = turn // block_len + 2
    cut = jnp.clip(lens[:, None] - block * block_len, 0, block_len)
    beyond = block - lens[:, None] // block_len
    beyond = jnp.where(
        jnp.logical_and(beyond >= 0, beyond < fresh_blocks - 1), beyond, fresh_blocks - 1
    )
    fill = beyond + fresh_blocks * jnp.arange(seats, dtype=jnp.int32)[:, None]
    at = leave[None, :] == jnp.arange(seats * max_blocks, dtype=jnp.int32)[:, None]
    by_leave = lambda per_block: jnp.sum(jnp.where(at, per_block.reshape(1, -1), 0), axis=1)
    merge_rows, merge_cut, merge_fill = by_leave(arrival), by_leave(cut), by_leave(fill)

    blank = jnp.zeros((kvh_dev, fresh_blocks * block_len, width), new_kv.dtype)
    fresh = jnp.stack(
        [
            lax.dynamic_update_slice(blank, new_kv[seat], (0, lens[seat] % block_len, 0))
            for seat in range(seats)
        ]
    ).reshape(seats, kvh_dev, fresh_blocks, block_len, width)

    new_group, new_rank = pool_places(new_slots, session_group, my_index, pool_dev, share)
    sender = new_group[:, None] * tp_count + jnp.arange(tp_count, dtype=jnp.int32)[None, :]
    store_rows = (sender * share + new_rank[:, None]).reshape(-1)

    query_t = jnp.swapaxes(
        queries.reshape(seats, kvh_dev, group_size * turn, head_dim), 2, 3
    )
    received = [
        lax.all_to_all(
            take(pool_rows, (first_row + slot).reshape(-1)).reshape(
                owners, share, block_len, width
            ),
            ("grp", "tp"),
            split_axis=0,
            concat_axis=0,
            tiled=True,
        )
        for slot in range(kvh_dev)
    ]
    grown, arrived, outputs = [], [], []
    for slot in range(kvh_dev):
        grown.append(
            merge(
                received[slot].reshape(owners * share, block_len, width),
                fresh[:, slot].reshape(seats * fresh_blocks, block_len, width),
                merge_rows,
                merge_cut,
                merge_fill,
            )
        )
        arrived.append(
            lax.all_to_all(
                grown[slot].reshape(owners, share, block_len, width),
                ("grp", "tp"),
                split_axis=0,
                concat_axis=0,
                tiled=True,
            )
        )
    for slot in range(kvh_dev):
        result = attend(grown[slot], query_t[:, slot], leave, lens, turn, max_blocks)
        outputs.append(jnp.swapaxes(result, 1, 2).reshape(seats, group_size, turn, head_dim))
    attention = jnp.concatenate(outputs, axis=1)
    pool = None
    pool_shape = (pool_dev, tp_count, kvh_dev, block_len, width)
    for slot in range(kvh_dev):
        blocks = arrived[slot].reshape(owners * share, block_len, width)
        pool = store(blocks, store_rows, pool, pool_shape, slot)
    return (attention, pool.reshape(kv_pool.shape))


def solution(mesh):
    in_specs = (
        P("grp", "tp", None, None),
        P("grp", "tp", None, None),
        P(("grp", "tp"), None, None, None),
        P(),
        P(),
        P(),
        P(),
    )
    out_specs = (P("grp", "tp", None, None), P(("grp", "tp"), None, None, None))
    return jax.shard_map(local, mesh=mesh, in_specs=in_specs, out_specs=out_specs, check_vma=False)
```

```python
import functools

import jax
import jax.numpy as jnp
from jax import lax
from jax.experimental import pallas as pl
from jax.experimental.pallas import tpu as pltpu
from jax.sharding import PartitionSpec as P

VMEM_LIMIT = 50 * 1024 * 1024


def merge_kernel(lanes, block_len, rows_ref, cut_ref, fresh_ref, *refs):
    cached_refs, fresh, out = refs[:lanes], refs[lanes], refs[lanes + 1]
    step = pl.program_id(0)
    for lane in range(lanes):
        cached = cached_refs[lane]
        cut = cut_ref[step * lanes + lane]
        fill = fresh_ref[step * lanes + lane]

        @pl.when(cut == block_len)
        def _():
            out[lane] = cached[0]

        @pl.when(cut == 0)
        def _():
            out[lane] = fresh[fill]

        @pl.when(jnp.logical_and(cut > 0, cut < block_len))
        def _():
            row = lax.broadcasted_iota(jnp.int32, cached.shape[1:], 0)
            out[lane] = jnp.where(
                row < cut, cached[0].astype(jnp.float32), fresh[fill].astype(jnp.float32)
            ).astype(out.dtype)


def merge(received, fresh, rows, cut, fill):
    total, block_len, width = received.shape
    lanes = 8
    spec = lambda lane: pl.BlockSpec(
        (1, block_len, width), lambda s, rows, cut, fill: (rows[s * lanes + lane], 0, 0)
    )
    return pl.pallas_call(
        functools.partial(merge_kernel, lanes, block_len),
        grid_spec=pltpu.PrefetchScalarGridSpec(
            num_scalar_prefetch=3,
            grid=(total // lanes,),
            in_specs=[spec(lane) for lane in range(lanes)]
            + [pl.BlockSpec(fresh.shape, lambda s, *_: (0, 0, 0))],
            out_specs=pl.BlockSpec((lanes, block_len, width), lambda s, *_: (s, 0, 0)),
        ),
        out_shape=jax.ShapeDtypeStruct(received.shape, received.dtype),
        compiler_params=pltpu.CompilerParams(vmem_limit_bytes=VMEM_LIMIT),
        cost_estimate=pl.CostEstimate(
            flops=0, bytes_accessed=4 * total * block_len * width, transcendentals=0
        ),
        name="merge_blocks",
    )(rows, cut, fill, *([received] * lanes), fresh)


def relay(sources, held, targets, arrive, leave):
    inward = [
        pltpu.make_async_copy(source, held.at[at], arrive.at[at])
        for at, source in enumerate(sources)
    ]
    outward = [
        pltpu.make_async_copy(held.at[at], target, leave.at[at])
        for at, target in enumerate(targets)
    ]
    for copy in inward:
        copy.start()
    for copy, after in zip(inward, outward):
        copy.wait()
        after.start()
    for copy in outward:
        copy.wait()


def take_kernel(count, rows_ref, source, out, held, arrive, leave):
    relay(
        [source.at[rows_ref[at]] for at in range(count)],
        held,
        [out.at[at] for at in range(count)],
        arrive,
        leave,
    )


def take(source, rows):
    count = rows.shape[0]
    shape = (count,) + source.shape[1:]
    return pl.pallas_call(
        functools.partial(take_kernel, count),
        grid_spec=pltpu.PrefetchScalarGridSpec(
            num_scalar_prefetch=1,
            grid=(1,),
            in_specs=[pl.BlockSpec(memory_space=pl.ANY)],
            out_specs=pl.BlockSpec(memory_space=pl.ANY),
            scratch_shapes=[
                pltpu.VMEM(shape, source.dtype),
                pltpu.SemaphoreType.DMA((count,)),
                pltpu.SemaphoreType.DMA((count,)),
            ],
        ),
        out_shape=jax.ShapeDtypeStruct(shape, source.dtype),
        compiler_params=pltpu.CompilerParams(vmem_limit_bytes=VMEM_LIMIT),
        cost_estimate=pl.CostEstimate(
            flops=0, bytes_accessed=4 * count * source.shape[1] * source.shape[2], transcendentals=0
        ),
        name="take_blocks",
    )(rows, source)


def store_kernel(pool_dev, heads, head_slot, rows_ref, arrived, *refs):
    out, held, arrive, leave = refs[-4:]
    places = [(slot, head) for slot in range(pool_dev) for head in range(heads)]
    relay(
        [arrived.at[rows_ref[slot * heads + head]] for slot, head in places],
        held,
        [out.at[slot, head, head_slot] for slot, head in places],
        arrive,
        leave,
    )


def store(arrived, rows, pool, pool_shape, head_slot):
    pool_dev, heads = pool_shape[:2]
    operands = [arrived]
    aliases = {}
    if pool is not None:
        operands.append(pool)
        aliases = {2: 0}
    return pl.pallas_call(
        functools.partial(store_kernel, pool_dev, heads, head_slot),
        grid_spec=pltpu.PrefetchScalarGridSpec(
            num_scalar_prefetch=1,
            grid=(1,),
            in_specs=[pl.BlockSpec(memory_space=pl.ANY)] * len(operands),
            out_specs=pl.BlockSpec(memory_space=pl.ANY),
            scratch_shapes=[
                pltpu.VMEM((pool_dev * heads,) + arrived.shape[1:], arrived.dtype),
                pltpu.SemaphoreType.DMA((pool_dev * heads,)),
                pltpu.SemaphoreType.DMA((pool_dev * heads,)),
            ],
        ),
        out_shape=jax.ShapeDtypeStruct(pool_shape, arrived.dtype),
        input_output_aliases=aliases,
        compiler_params=pltpu.CompilerParams(vmem_limit_bytes=VMEM_LIMIT),
        cost_estimate=pl.CostEstimate(
            flops=0, bytes_accessed=4 * arrived.size, transcendentals=0
        ),
        name="store_blocks",
    )(rows, *operands)


def attend_kernel(pages, block_len, turn, tile, scale, places_ref, lens_ref, *refs):
    page_refs = refs[:pages]
    query, out, total, high, norm = refs[pages:]
    seat, step = pl.program_id(0), pl.program_id(1)
    head_dim, rows = query.shape[1:]
    span = pages * block_len
    length = lens_ref[seat]
    base = step * span
    factor = scale * 1.4426950408889634

    @pl.when(step == 0)
    def _():
        total[...] = jnp.zeros_like(total)
        norm[...] = jnp.zeros_like(norm)
        high[...] = jnp.full_like(high, -1e30)

    def update(masked):
        keys = jnp.concatenate([page[0, :, :head_dim] for page in page_refs], axis=0)
        values = jnp.concatenate([page[0, :, head_dim:] for page in page_refs], axis=0)
        values_t = values.T
        for at in range(0, rows, tile):
            part = pl.ds(at, tile)
            scores = jnp.dot(keys, query[0, :, part], preferred_element_type=jnp.float32)
            if masked:
                column = lax.broadcasted_iota(jnp.int32, scores.shape, 0) + base
                limit = (lax.broadcasted_iota(jnp.int32, scores.shape, 1) + at) % turn + length
                scores = jnp.where(column <= limit, scores, -1e30)
            before = high[:, part]
            now = jnp.maximum(before, jnp.max(scores, axis=0, keepdims=True))
            weights = jnp.exp2((scores - now) * factor)
            fade = jnp.exp2((before - now) * factor)
            high[:, part] = now
            norm[:, part] = norm[:, part] * fade + jnp.sum(weights, axis=0, keepdims=True)
            total[:, part] = total[:, part] * fade + jnp.dot(
                values_t, weights.astype(jnp.bfloat16), preferred_element_type=jnp.float32
            )

    @pl.when(base + span - 1 <= length)
    def _():
        update(False)

    @pl.when(jnp.logical_and(base + span - 1 > length, base < length + turn))
    def _():
        update(True)

    @pl.when(step == pl.num_programs(1) - 1)
    def _():
        out[0] = (total[...] / norm[...]).astype(out.dtype)


def attend(grown, query_t, places, lens, turn, max_blocks):
    seats, head_dim, rows = query_t.shape
    unused_total, block_len, width = grown.shape
    pages = 4
    span = pages * block_len
    steps = max_blocks // pages

    def spec(page):
        def index(seat, step, places, lens):
            last = (lens[seat] + turn - 1) // span
            return (places[seat * max_blocks + jnp.minimum(step, last) * pages + page], 0, 0)

        return pl.BlockSpec((1, block_len, width), index)

    by_seat = pl.BlockSpec((1, head_dim, rows), lambda seat, step, *_: (seat, 0, 0))
    work = seats * rows * max_blocks * block_len
    return pl.pallas_call(
        functools.partial(
            attend_kernel, pages, block_len, turn, min(512, rows), head_dim ** (-0.5)
        ),
        grid_spec=pltpu.PrefetchScalarGridSpec(
            num_scalar_prefetch=2,
            grid=(seats, steps),
            in_specs=[spec(page) for page in range(pages)] + [by_seat],
            out_specs=by_seat,
            scratch_shapes=[
                pltpu.VMEM((head_dim, rows), jnp.float32),
                pltpu.VMEM((1, rows), jnp.float32),
                pltpu.VMEM((1, rows), jnp.float32),
            ],
        ),
        out_shape=jax.ShapeDtypeStruct(query_t.shape, query_t.dtype),
        compiler_params=pltpu.CompilerParams(vmem_limit_bytes=VMEM_LIMIT),
        cost_estimate=pl.CostEstimate(
            flops=4 * work * head_dim, bytes_accessed=2 * grown.size, transcendentals=work
        ),
        name="attend_head",
    )(places, lens, *([grown] * pages), query_t)


def pool_places(slots, session_group, my_index, pool_dev, share):
    mine = my_index * pool_dev + jnp.arange(pool_dev, dtype=jnp.int32)
    match = slots[None] == mine[:, None, None]
    group = jnp.sum(jnp.where(match, session_group[None, :, None], 0), axis=(1, 2))
    local = jnp.arange(pool_dev, dtype=jnp.int32)
    earlier = jnp.logical_and(group[None, :] == group[:, None], local[None, :] < local[:, None])
    return group, jnp.sum(earlier.astype(jnp.int32), axis=1)


def group_places(table, pool_dev, share):
    slots = table.reshape(-1)
    owner = slots // pool_dev
    earlier = jnp.logical_and(owner[None, :] == owner[:, None], slots[None, :] < slots[:, None])
    return owner * share + jnp.sum(earlier.astype(jnp.int32), axis=1)


def local(queries, new_kv, kv_pool, cache_lens, session_seat, old_slots, new_slots):
    group_count = lax.axis_size("grp")
    tp_count = lax.axis_size("tp")
    owners = group_count * tp_count
    pool_dev, kv_heads, block_len, width = kv_pool.shape
    head_dim = width // 2
    seats, qh_dev, turn, unused_dim = queries.shape
    kvh_dev = new_kv.shape[1]
    group_size = qh_dev // kvh_dev
    max_blocks = old_slots.shape[1]
    share = pool_dev // group_count
    group_index = lax.axis_index("grp")
    my_index = group_index * tp_count + lax.axis_index("tp")
    session_group = session_seat // seats

    group, rank = pool_places(old_slots, session_group, my_index, pool_dev, share)
    locals_ = jnp.arange(pool_dev, dtype=jnp.int32)
    order = jnp.sum(
        jnp.where((group * share + rank)[None, :] == locals_[:, None], locals_[None, :], 0), axis=1
    )
    pick = jnp.repeat(order.reshape(group_count, 1, share), tp_count, axis=1)
    head = jnp.arange(tp_count, dtype=jnp.int32)[None, :, None] * kvh_dev
    first_row = (pick * kv_heads + head).reshape(owners, share)
    pool_rows = kv_pool.reshape(pool_dev * kv_heads, block_len, width)

    seat_ids = group_index * seats + jnp.arange(seats, dtype=jnp.int32)
    here = session_seat[None, :] == seat_ids[:, None]
    lens = jnp.sum(jnp.where(here, cache_lens[None, :], 0), axis=1)
    old_table = jnp.sum(jnp.where(here[:, :, None], old_slots[None], 0), axis=1)
    new_table = jnp.sum(jnp.where(here[:, :, None], new_slots[None], 0), axis=1)
    arrival = group_places(old_table, pool_dev, share)
    leave = group_places(new_table, pool_dev, share)
    block = jnp.arange(max_blocks, dtype=jnp.int32)[None, :]
    fresh_blocks = turn // block_len + 2
    cut = jnp.clip(lens[:, None] - block * block_len, 0, block_len)
    beyond = block - lens[:, None] // block_len
    beyond = jnp.where(
        jnp.logical_and(beyond >= 0, beyond < fresh_blocks - 1), beyond, fresh_blocks - 1
    )
    fill = beyond + fresh_blocks * jnp.arange(seats, dtype=jnp.int32)[:, None]
    at = leave[None, :] == jnp.arange(seats * max_blocks, dtype=jnp.int32)[:, None]
    by_leave = lambda per_block: jnp.sum(jnp.where(at, per_block.reshape(1, -1), 0), axis=1)
    merge_rows, merge_cut, merge_fill = by_leave(arrival), by_leave(cut), by_leave(fill)

    blank = jnp.zeros((kvh_dev, fresh_blocks * block_len, width), new_kv.dtype)
    fresh = jnp.stack(
        [
            lax.dynamic_update_slice(blank, new_kv[seat], (0, lens[seat] % block_len, 0))
            for seat in range(seats)
        ]
    ).reshape(seats, kvh_dev, fresh_blocks, block_len, width)

    new_group, new_rank = pool_places(new_slots, session_group, my_index, pool_dev, share)
    sender = new_group[:, None] * tp_count + jnp.arange(tp_count, dtype=jnp.int32)[None, :]
    store_rows = (sender * share + new_rank[:, None]).reshape(-1)

    query_t = jnp.swapaxes(
        queries.reshape(seats, kvh_dev, group_size * turn, head_dim), 2, 3
    )
    received = [
        lax.all_to_all(
            take(pool_rows, (first_row + slot).reshape(-1)).reshape(
                owners, share, block_len, width
            ),
            ("grp", "tp"),
            split_axis=0,
            concat_axis=0,
            tiled=True,
        )
        for slot in range(kvh_dev)
    ]
    grown, arrived, outputs = [], [], []
    for slot in range(kvh_dev):
        grown.append(
            merge(
                received[slot].reshape(owners * share, block_len, width),
                fresh[:, slot].reshape(seats * fresh_blocks, block_len, width),
                merge_rows,
                merge_cut,
                merge_fill,
            )
        )
        arrived.append(
            lax.all_to_all(
                grown[slot].reshape(owners, share, block_len, width),
                ("grp", "tp"),
                split_axis=0,
                concat_axis=0,
                tiled=True,
            )
        )
    for slot in range(kvh_dev):
        result = attend(grown[slot], query_t[:, slot], leave, lens, turn, max_blocks)
        outputs.append(jnp.swapaxes(result, 1, 2).reshape(seats, group_size, turn, head_dim))
    attention = jnp.concatenate(outputs, axis=1)
    pool = None
    pool_shape = (pool_dev, tp_count, kvh_dev, block_len, width)
    for slot in range(kvh_dev):
        blocks = arrived[slot].reshape(owners * share, block_len, width)
        pool = store(blocks, store_rows, pool, pool_shape, slot)
    return (attention, pool.reshape(kv_pool.shape))


def solution(mesh):
    in_specs = (
        P("grp", "tp", None, None),
        P("grp", "tp", None, None),
        P(("grp", "tp"), None, None, None),
        P(),
        P(),
        P(),
        P(),
    )
    out_specs = (P("grp", "tp", None, None), P(("grp", "tp"), None, None, None))
    return jax.shard_map(local, mesh=mesh, in_specs=in_specs, out_specs=out_specs, check_vma=False)
```
